32 devices in a mesh: dp: 8 (over z, y), fsdp: 4 (over x, core).
Axes of the slice: x: 2, y: 2, z: 4, core: 2. Of those that a mesh axis runs over, the one named last changes fastest.
Arguments:
- student_frames: bfloat16 [16384, 1024], P(('dp', 'fsdp')), may hold values from -6 to 6
- teacher_layers: bfloat16 [2, 16384, 1024], P(None, ('dp', 'fsdp')), as said below
- mask_blocks: int32 [32, 32], P(('dp', 'fsdp')), may hold values from 0 to 63, as said below
- w_in: bfloat16 [384, 1024], P('fsdp'), may hold values from -6 to 6
- w_out: bfloat16 [384, 1024], P('fsdp'), may hold values from -6 to 6
- teacher_in: float32 [384, 1024], P('fsdp'), may hold values from -6 to 6
- teacher_out: float32 [384, 1024], P('fsdp'), may hold values from -6 to 6
Outputs:
- grad_in: float32 [384, 1024], P('fsdp')
- grad_out: float32 [384, 1024], P('fsdp')
- new_teacher_in: float32 [384, 1024], P('fsdp')
- new_teacher_out: float32 [384, 1024], P('fsdp')
The draws below stay inside these ranges and needn't reach their ends.
Inputs may be any that keep to these rules, and one draw needn't show every extreme that they name: `mask_blocks`: each row holds 32 different block numbers. `teacher_layers`: finite values.
All inputs are finite; a program needn't handle non-finite values.
Results may differ from the reference program's by a relative error of at most 0.0029.
Values may be sent and summed in bfloat16 or wider, within the bound.
A program may use at most 64 MiB of HBM per device.

```python
import jax
import jax.numpy as jnp
from jax import lax

D = 1024
R = 384
K = 2
SPAN = 8
FRAMES = 512
NBLK = 64
NMASK = 32
UTTS = 32
TOKENS = 16384


def draw_mask_blocks(key, part):
    key = jax.random.fold_in(key, 7)
    row_keys = jax.random.split(key, UTTS)

    def one_row(row_key):
        return jax.random.permutation(row_key, NBLK)[:NMASK].astype(jnp.int32)
    return jax.vmap(one_row)(row_keys)


def draw_teacher_layers(key, part):
    key = jax.random.fold_in(key, 11)
    base_key, frame_key, channel_key, offset_key = jax.random.split(key, 4)
    full_shape = (K, TOKENS, D)
    frame_scale = jnp.exp(jax.random.uniform(frame_key, (K, TOKENS, 1), jnp.float32, 0.0, 2.3))
    channel_scale = jnp.exp(jax.random.uniform(channel_key, (K, 1, D), jnp.float32, -0.7, 0.7))
    noise_base = jax.random.normal(base_key, full_shape, jnp.float32)
    offsets = jax.random.normal(offset_key, (K, 1, D), jnp.float32)
    return (noise_base * frame_scale * channel_scale + offsets).astype(jnp.bfloat16)


def levels(stream_key, shape, cuts, low, top_value):
    loudness = 1.0
    for dim, blocks in cuts:
        steps = jax.random.uniform(jax.random.fold_in(jax.random.fold_in(stream_key, 6), dim), (blocks,), jnp.float32, low / len(cuts), top_value / len(cuts))
        loudness = loudness * jnp.repeat(jnp.exp(steps), shape[dim] // blocks).reshape((-1,) + (1,) * (len(shape) - 1 - dim))
    return loudness


def noise(stream_key, extent, scale, most, shards=(), held_as=jnp.bfloat16):
    gain = levels(stream_key, extent, shards, -0.22, 0.18) if shards else 1.0
    drawn = jax.random.normal(stream_key, extent, jnp.float32) * scale * gain
    return jnp.minimum(jnp.maximum(drawn, -most), most).astype(held_as)


def setup_inputs(seed: int = 0) -> dict:
    seeds = jax.random.split(jax.random.key(seed), 8)
    return {
        "student_frames": noise(seeds[0], (TOKENS, D), 1.0, 6.0, ((0, 32),)),
        "teacher_layers": draw_teacher_layers(jax.random.fold_in(seeds[7], 71), 0),
        "mask_blocks": draw_mask_blocks(jax.random.fold_in(seeds[7], 71), 0),
        "w_in": noise(seeds[3], (R, D), 1.0, 6.0, ((0, 4),)),
        "w_out": noise(seeds[4], (R, D), 1.0, 6.0, ((0, 4),)),
        "teacher_in": noise(seeds[5], (R, D), 1.0, 6.0, ((0, 4),), jnp.float32),
        "teacher_out": noise(seeds[6], (R, D), 1.0, 6.0, ((0, 4),), jnp.float32),
    }


def gelu_fn(inputs):
    return jax.nn.gelu(inputs, approximate=True)

def targets_of(layers):
    values = layers.astype(jnp.float32)
    center = values - lax.optimization_barrier(jnp.mean(values, axis=1, keepdims=True))
    spread = lax.optimization_barrier(jnp.mean(center * center, axis=1, keepdims=True))
    return lax.optimization_barrier(jnp.mean(center / jnp.sqrt(spread + 1e-05), axis=0))

def frame_mask(blocks, frames):
    block_of = jnp.arange(frames, dtype=jnp.int32) // SPAN
    matches = block_of[:, None] == blocks[None, :].astype(jnp.int32)
    return jnp.any(matches, axis=1).astype(jnp.float32)

def local_terms(frames_here, layers, blocks, full_in, full_out, total_masked):
    model_width = full_in.shape[1]
    hidden = full_in.shape[0]
    before = lax.dot_general(frames_here, full_in, (((1,), (1,)), ((), ())), preferred_element_type=jnp.float32) * model_width ** (-0.5)
    active, pullback = jax.vjp(gelu_fn, before)
    active_low = active.astype(jnp.bfloat16)
    predicted = jnp.dot(active_low, full_out, preferred_element_type=jnp.float32) * hidden ** (-0.5)
    target = targets_of(layers)
    masked = frame_mask(blocks, frames_here.shape[0])
    scaled_error = (masked[:, None] * (predicted - target) * (hidden / total_masked) ** 0.5).astype(jnp.bfloat16)
    term_out = (lax.dot_general(active_low, scaled_error, (((0,), (0,)), ((), ())), preferred_element_type=jnp.float32) * hidden ** (-0.5)).astype(jnp.bfloat16)
    backward = lax.dot_general(scaled_error, full_out, (((1,), (1,)), ((), ())), preferred_element_type=jnp.float32) * hidden ** (-0.5)
    grad_before = pullback(backward)[0].astype(jnp.bfloat16)
    term_in = (lax.dot_general(grad_before, frames_here, (((0,), (0,)), ((), ())), preferred_element_type=jnp.float32) * model_width ** (-0.5)).astype(jnp.bfloat16)
    return (term_in, term_out)

def reference(student_frames, teacher_layers, mask_blocks, w_in, w_out, teacher_in, teacher_out):
    total_masked = UTTS * NMASK * SPAN

    def advance(totals, utterance):
        offset = (utterance * FRAMES).astype(jnp.int32)
        frames_here = lax.dynamic_slice_in_dim(student_frames, offset, FRAMES, 0)
        layers = lax.dynamic_slice_in_dim(teacher_layers, offset, FRAMES, 1)
        blocks = lax.dynamic_slice_in_dim(mask_blocks, utterance.astype(jnp.int32), 1, 0)[0]
        term_in, term_out = local_terms(frames_here, layers, blocks, w_in, w_out, total_masked)
        return ((totals[0] + term_in.astype(jnp.float32), totals[1] + term_out.astype(jnp.float32)), None)
    empty_sum = jnp.zeros((R, D), jnp.float32)
    (grad_in, grad_out), _ = lax.scan(advance, (empty_sum, empty_sum), jnp.arange(UTTS, dtype=jnp.int32))
    ema_decay = 0.999
    new_in = ema_decay * teacher_in + (1.0 - ema_decay) * w_in.astype(jnp.float32)
    new_out = ema_decay * teacher_out + (1.0 - ema_decay) * w_out.astype(jnp.float32)
    return (grad_in, grad_out, new_in, new_out)
```

```python
import functools

import jax
import jax.numpy as jnp
from jax import lax
from jax.experimental import pallas as pl
from jax.experimental.pallas import tpu as pltpu
from jax.sharding import PartitionSpec as P

MESH = pl.DeviceIdType.MESH

SPAN = 8


def gelu_fn(inputs):
    return jax.nn.gelu(inputs, approximate=True)


def targets_of(layers):
    values = layers.astype(jnp.float32)
    center = values - jnp.mean(values, axis=1, keepdims=True)
    spread = jnp.mean(center * center, axis=1, keepdims=True)
    return jnp.mean(center / jnp.sqrt(spread + 1e-05), axis=0)


def frame_mask(blocks, frames):
    block_of = jnp.arange(frames, dtype=jnp.int32) // SPAN
    matches = block_of[:, None] == blocks[None, :]
    return jnp.any(matches, axis=1).astype(jnp.float32)


def local_terms(frames_here, layers, blocks, full_in, full_out, total_masked):
    model_width = full_in.shape[1]
    hidden = full_in.shape[0]
    before = lax.dot_general(
        frames_here, full_in, (((1,), (1,)), ((), ())), preferred_element_type=jnp.float32
    ) * model_width ** (-0.5)
    active, pullback = jax.vjp(gelu_fn, before)
    active_low = active.astype(jnp.bfloat16)
    predicted = jnp.dot(active_low, full_out, preferred_element_type=jnp.float32) * hidden ** (-0.5)
    target = targets_of(layers)
    masked = frame_mask(blocks, frames_here.shape[0])
    scaled_error = (masked[:, None] * (predicted - target) * (hidden / total_masked) ** 0.5).astype(
        jnp.bfloat16
    )
    term_out = (
        lax.dot_general(
            active_low, scaled_error, (((0,), (0,)), ((), ())), preferred_element_type=jnp.float32
        )
        * hidden ** (-0.5)
    ).astype(jnp.bfloat16)
    backward = lax.dot_general(
        scaled_error, full_out, (((1,), (1,)), ((), ())), preferred_element_type=jnp.float32
    ) * hidden ** (-0.5)
    grad_before = pullback(backward)[0].astype(jnp.bfloat16)
    term_in = (
        lax.dot_general(
            grad_before, frames_here, (((0,), (0,)), ((), ())), preferred_element_type=jnp.float32
        )
        * model_width ** (-0.5)
    ).astype(jnp.bfloat16)
    return (term_in, term_out)


ROOT_2_PI = 0.7978845608028654
CUBIC = 0.044715


def head_kernel(
    scale_error,
    frames_hbm, layers_hbm, mask_ref, w_in_ref, w_out_ref,
    grad_ref,
    frames, layers, target, full_in, full_out, active_t, slope_t, error, grad_t,
    term, pair_in, x_out, x_in, y_out, y_in, kept, half_kept, z_out, z_in, z_kept, whole,
    local_sem, w_send, w_recv, g_send, g_recv,
):
    f = lax.axis_index("fsdp")
    d = lax.axis_index("dp")
    x, c = f // 2, f % 2
    z, y = d // 2, d % 2
    sibling = {"dp": d, "fsdp": 2 * x + (1 - c)}
    x_peer = {"dp": d, "fsdp": 2 * (1 - x) + c}
    y_peer = {"dp": 2 * z + (1 - y), "fsdp": f}
    z_peers = [{"dp": 2 * ((z + j) % 4) + y, "fsdp": f} for j in (1, 2, 3)]
    far = 2 * (1 - x) + c

    loads = [
        pltpu.make_async_copy(layers_hbm, layers, local_sem.at[0]),
        pltpu.make_async_copy(frames_hbm, frames, local_sem.at[1]),
        pltpu.make_async_copy(w_in_ref, full_in.at[f], local_sem.at[2]),
        pltpu.make_async_copy(w_out_ref, full_out.at[f], local_sem.at[3]),
    ]
    for load in loads:
        load.start()

    barrier = pltpu.get_barrier_semaphore()
    peers = [sibling, x_peer, y_peer] + z_peers
    for peer in peers:
        pl.semaphore_signal(barrier, inc=1, device_id=peer, device_id_type=MESH)
    pl.semaphore_wait(barrier, len(peers))

    pending = []

    def remote(src, dst, send, recv, peer):
        copy = pltpu.make_async_remote_copy(
            src_ref=src, dst_ref=dst, send_sem=send, recv_sem=recv,
            device_id=peer, device_id_type=MESH,
        )
        copy.start()
        pending.append(copy)
        return copy

    shards = ((w_in_ref, full_in), (w_out_ref, full_out))
    over_x, to_sibling = [], []
    for k, (shard, full) in enumerate(shards):
        over_x.append(remote(shard.at[y], full.at[f, y], w_send.at[k, 0], w_recv.at[k, 0], x_peer))
    for k, (shard, full) in enumerate(shards):
        to_sibling.append([remote(shard, full.at[f], w_send.at[k, 1], w_recv.at[k, 1], sibling)])

    over_y = []

    def forward_x(k):
        full = shards[k][1]
        over_x[k].wait_recv()
        over_y.append(remote(full.at[far, y], full.at[far, y], w_send.at[k, 2], w_recv.at[k, 2], y_peer))
        to_sibling[k].append(
            remote(full.at[far, y], full.at[far, y], w_send.at[k, 3], w_recv.at[k, 3], sibling)
        )

    def forward_y(k):
        full = shards[k][1]
        over_y[k].wait_recv()
        to_sibling[k].append(
            remote(full.at[far, 1 - y], full.at[far, 1 - y], w_send.at[k, 4], w_recv.at[k, 4], sibling)
        )

    count, width = frames.shape
    def targets(first, last):
        for start in range(first, last, 128):
            total = None
            for layer in range(2):
                v = layers[layer, :, start:start + 128].astype(jnp.float32)
                center = v - jnp.mean(v, axis=0, keepdims=True)
                spread = jnp.mean(center * center, axis=0, keepdims=True)
                part = center * (0.5 / jnp.sqrt(spread + 1e-05))
                total = part if total is None else total + part
            target[:, start:start + 128] = total

    loads[0].wait()
    targets(0, width // 2)
    forward_x(0)
    targets(width // 2, 3 * width // 4)
    forward_y(0)
    forward_x(1)
    targets(3 * width // 4, width)
    block_of = lax.broadcasted_iota(jnp.int32, (count, mask_ref.shape[1]), 0) // SPAN
    hits = jnp.where(block_of == mask_ref[...], 1.0, 0.0)
    masked = jnp.max(hits, axis=1, keepdims=True)
    loads[1].wait()
    loads[2].wait()
    for copy in to_sibling[0]:
        copy.wait_recv()

    hidden = 8 * full_in.shape[2]
    rows = hidden // 8
    in_all = full_in[...].reshape(hidden, width)
    before = lax.dot_general(
        in_all, frames[...], (((1,), (1,)), ((), ())), preferred_element_type=jnp.float32
    ) * width ** (-0.5)
    bend = jnp.tanh(ROOT_2_PI * (before + CUBIC * before * before * before))
    active_t[...] = (before * (0.5 * (1.0 + bend))).astype(jnp.bfloat16)
    slope_t[...] = 0.5 * (1.0 + bend) + (0.5 * ROOT_2_PI) * before * (1.0 - bend * bend) * (
        1.0 + 3.0 * CUBIC * before * before
    )

    forward_y(1)
    loads[3].wait()
    for copy in to_sibling[1]:
        copy.wait_recv()
    active = active_t[...].T

    half = width // 2

    def errors(start):
        for at in range(start, start + half, 256):
            predicted = jnp.dot(
                active, full_out[:, :, :, at:at + 256].reshape(hidden, 256),
                preferred_element_type=jnp.float32,
            ) * hidden ** (-0.5)
            error[:, at:at + 256] = (
                masked * (predicted - target[:, at:at + 256]) * scale_error
            ).astype(jnp.bfloat16)

    sent = {}

    def send_pair(s, value):
        value = value.astype(jnp.bfloat16)
        for i in range(8):
            term[s, i // 2, i % 2] = value[i * rows:(i + 1) * rows]
        sent[s, "pair"] = [
            remote(term.at[s, 2 * i + (1 - c)], pair_in.at[s, i], g_send.at[s, i], g_recv.at[s, i], sibling)
            for i in range(2)
        ]

    def wide(value):
        return value.astype(jnp.float32)

    def send_x(s, ref):
        return [remote(ref[0], ref[1], g_send.at[s, 2], g_recv.at[s, 2], x_peer)]

    def send_y(s, ref):
        return [remote(ref[0], ref[1], g_send.at[s, 3], g_recv.at[s, 3], y_peer)]

    def arrived(s, name):
        for copy in sent[s, name]:
            copy.wait_recv()

    def first(s):
        arrived(s, "pair")
        if s < 2:
            x_out[s] = (wide(term[s, far]) + wide(pair_in[s, 1 - x])).astype(jnp.bfloat16)
            sent[s, "first"] = send_x(s, (x_out.at[s], x_in.at[s]))
            kept[s] = wide(term[s, f]) + wide(pair_in[s, x])
        else:
            for i in range(2):
                y_out[s, i] = (
                    wide(term[s, 2 * i + c, 1 - y]) + wide(pair_in[s, i, 1 - y])
                ).astype(jnp.bfloat16)
            sent[s, "first"] = send_y(s, (y_out.at[s], y_in.at[s]))
            for i in range(2):
                kept[s, i] = wide(term[s, 2 * i + c, y]) + wide(pair_in[s, i, y])

    def second(s):
        arrived(s, "first")
        if s < 2:
            y_out[s, 0] = (kept[s, 1 - y] + wide(x_in[s, 1 - y])).astype(jnp.bfloat16)
            sent[s, "second"] = send_y(s, (y_out.at[s, 0], y_in.at[s, 0]))
            half_kept[s] = kept[s, y] + wide(x_in[s, y])
        else:
            x_out[s, 0] = (kept[s, 1 - x] + wide(y_in[s, 1 - x])).astype(jnp.bfloat16)
            sent[s, "second"] = send_x(s, (x_out.at[s, 0], x_in.at[s, 0]))
            half_kept[s] = kept[s, x] + wide(y_in[s, x])

    quarter = half // 4

    def third(s):
        arrived(s, "second")
        total = half_kept[s] + wide(y_in[s, 0] if s < 2 else x_in[s, 0])
        for q in range(4):
            part = total[:, q * quarter:(q + 1) * quarter]
            z_out[s, q] = part.astype(jnp.bfloat16)
            z_kept[s, q] = part
        sent[s, "third"] = [
            remote(
                z_out.at[s, (z + j) % 4], z_in.at[s, j - 1],
                g_send.at[s, 3 + j], g_recv.at[s, 3 + j], z_peers[j - 1],
            )
            for j in (1, 2, 3)
        ]

    def fourth(s):
        arrived(s, "third")
        total = z_kept[s, z] + wide(z_in[s, 0]) + wide(z_in[s, 1]) + wide(z_in[s, 2])
        whole[s, y, z] = total.astype(jnp.bfloat16)
        sent[s, "fourth"] = [
            remote(
                whole.at[s, y, z], whole.at[s, y, z],
                g_send.at[s, 6 + j], g_recv.at[s, 6 + j], z_peers[j - 1],
            )
            for j in (1, 2, 3)
        ]

    def fifth(s):
        arrived(s, "fourth")
        sent[s, "fifth"] = [
            remote(whole.at[s, y], whole.at[s, y], g_send.at[s, 10], g_recv.at[s, 10], y_peer)
        ]

    def last(s):
        arrived(s, "fifth")
        for h in range(2):
            for q in range(4):
                at = (s % 2) * half + q * quarter
                grad_ref[s // 2, h * rows:(h + 1) * rows, at:at + quarter] = whole[s, h, q]

    for s in range(2):
        at = s * half
        errors(at)
        send_pair(
            s,
            jnp.dot(active_t[...], error[:, at:at + half], preferred_element_type=jnp.float32)
            * hidden ** (-0.5),
        )
    first(0)
    backward = lax.dot_general(
        full_out[...].reshape(hidden, width), error[...], (((1,), (1,)), ((), ())),
        preferred_element_type=jnp.float32,
    ) * hidden ** (-0.5)
    grad_t[...] = (slope_t[...] * backward).astype(jnp.bfloat16)
    first(1)
    for s in range(2, 4):
        at = (s - 2) * half
        send_pair(
            s,
            jnp.dot(grad_t[...], frames[:, at:at + half], preferred_element_type=jnp.float32)
            * width ** (-0.5),
        )
    first(2)
    first(3)
    for step in (second, third, fourth, fifth, last):
        for s in (0, 2, 1, 3):
            step(s)
    for copy in pending:
        copy.wait_send()


def head_call(student_frames, teacher_layers, mask_blocks, w_in, w_out, scale_error):
    count, width = student_frames.shape
    shard = w_in.shape[0]
    hidden = 4 * shard
    rows, half, quarter = shard // 2, width // 2, width // 8
    low, f32 = jnp.bfloat16, jnp.float32
    anywhere = pl.BlockSpec(memory_space=pl.ANY)
    inside = pl.BlockSpec(memory_space=pltpu.VMEM)
    return pl.pallas_call(
        functools.partial(head_kernel, scale_error),
        out_shape=jax.ShapeDtypeStruct((2, shard, width), low),
        in_specs=[anywhere, anywhere, inside, anywhere, anywhere],
        out_specs=inside,
        scratch_shapes=[
            pltpu.VMEM((count, width), low),
            pltpu.VMEM((2, count, width), low),
            pltpu.VMEM((count, width), f32),
            pltpu.VMEM((4, 2, rows, width), low),
            pltpu.VMEM((4, 2, rows, width), low),
            pltpu.VMEM((hidden, count), low),
            pltpu.VMEM((hidden, count), f32),
            pltpu.VMEM((count, width), low),
            pltpu.VMEM((hidden, count), low),
            pltpu.VMEM((4, 4, 2, rows, half), low),
            pltpu.VMEM((4, 2, 2, rows, half), low),
            pltpu.VMEM((4, 2, rows, half), low),
            pltpu.VMEM((4, 2, rows, half), low),
            pltpu.VMEM((4, 2, rows, half), low),
            pltpu.VMEM((4, 2, rows, half), low),
            pltpu.VMEM((4, 2, rows, half), f32),
            pltpu.VMEM((4, rows, half), f32),
            pltpu.VMEM((4, 4, rows, quarter), low),
            pltpu.VMEM((4, 3, rows, quarter), low),
            pltpu.VMEM((4, 4, rows, quarter), f32),
            pltpu.VMEM((4, 2, 4, rows, quarter), low),
            pltpu.SemaphoreType.DMA((4,)),
            pltpu.SemaphoreType.DMA((2, 5)),
            pltpu.SemaphoreType.DMA((2, 5)),
            pltpu.SemaphoreType.DMA((4, 11)),
            pltpu.SemaphoreType.DMA((4, 11)),
        ],
        compiler_params=pltpu.CompilerParams(
            collective_id=0, has_side_effects=True, vmem_limit_bytes=48 * 1024 * 1024
        ),
        cost_estimate=pl.CostEstimate(
            flops=10 * count * hidden * width,
            bytes_accessed=6 * count * width + 4 * hidden * width,
            transcendentals=count * hidden,
        ),
    )(
        student_frames, teacher_layers, mask_blocks,
        w_in.reshape(2, rows, width), w_out.reshape(2, rows, width),
    )


def averaged(w_in, w_out, teacher_in, teacher_out):
    ema_decay = 0.999
    new_in = ema_decay * teacher_in + (1.0 - ema_decay) * w_in.astype(jnp.float32)
    new_out = ema_decay * teacher_out + (1.0 - ema_decay) * w_out.astype(jnp.float32)
    return (new_in, new_out)


def body(student_frames, teacher_layers, mask_blocks, w_in, w_out, teacher_in, teacher_out):
    fused = lax.axis_size("fsdp") == 4 and lax.axis_size("dp") == 8
    if fused:
        total_masked = 32 * mask_blocks.shape[1] * SPAN
        grads = head_call(
            student_frames, teacher_layers, mask_blocks, w_in, w_out,
            (4 * w_in.shape[0] / total_masked) ** 0.5,
        ).astype(jnp.float32)
        return (grads[1], grads[0]) + averaged(w_in, w_out, teacher_in, teacher_out)
    full_in, full_out = (
        lax.all_gather(w_in, "fsdp", axis=0, tiled=True),
        lax.all_gather(w_out, "fsdp", axis=0, tiled=True),
    )
    count_dp = lax.axis_size("dp")
    count_fsdp = lax.axis_size("fsdp")
    total_masked = count_dp * count_fsdp * mask_blocks.shape[1] * SPAN
    term_in, term_out = local_terms(
        student_frames, teacher_layers, mask_blocks[0], full_in, full_out, total_masked
    )
    summands = (term_in.astype(jnp.float32), term_out.astype(jnp.float32))
    shards = (
        lax.psum_scatter(summands[0], "fsdp", scatter_dimension=0, tiled=True),
        lax.psum_scatter(summands[1], "fsdp", scatter_dimension=0, tiled=True),
    )
    grad_in, grad_out = lax.psum((shards[0], shards[1]), "dp")
    return (grad_in, grad_out) + averaged(w_in, w_out, teacher_in, teacher_out)


def solution(mesh):
    return jax.shard_map(
        body,
        mesh=mesh,
        in_specs=(
            P(("dp", "fsdp"), None),
            P(None, ("dp", "fsdp"), None),
            P(("dp", "fsdp"), None),
            P("fsdp", None),
            P("fsdp", None),
            P("fsdp", None),
            P("fsdp", None),
        ),
        out_specs=(P("fsdp", None), P("fsdp", None), P("fsdp", None), P("fsdp", None)),
        check_vma=False,
    )
```

```python
import functools

import jax
import jax.numpy as jnp
from jax import lax
from jax.experimental import pallas as pl
from jax.experimental.pallas import tpu as pltpu
from jax.sharding import PartitionSpec as P

MESH = pl.DeviceIdType.MESH

SPAN = 8


def gelu_fn(inputs):
    return jax.nn.gelu(inputs, approximate=True)


def targets_of(layers):
    values = layers.astype(jnp.float32)
    center = values - jnp.mean(values, axis=1, keepdims=True)
    spread = jnp.mean(center * center, axis=1, keepdims=True)
    return jnp.mean(center / jnp.sqrt(spread + 1e-05), axis=0)


def frame_mask(blocks, frames):
    block_of = jnp.arange(frames, dtype=jnp.int32) // SPAN
    matches = block_of[:, None] == blocks[None, :]
    return jnp.any(matches, axis=1).astype(jnp.float32)


def local_terms(frames_here, layers, blocks, full_in, full_out, total_masked):
    model_width = full_in.shape[1]
    hidden = full_in.shape[0]
    before = lax.dot_general(
        frames_here, full_in, (((1,), (1,)), ((), ())), preferred_element_type=jnp.float32
    ) * model_width ** (-0.5)
    active, pullback = jax.vjp(gelu_fn, before)
    active_low = active.astype(jnp.bfloat16)
    predicted = jnp.dot(active_low, full_out, preferred_element_type=jnp.float32) * hidden ** (-0.5)
    target = targets_of(layers)
    masked = frame_mask(blocks, frames_here.shape[0])
    scaled_error = (masked[:, None] * (predicted - target) * (hidden / total_masked) ** 0.5).astype(
        jnp.bfloat16
    )
    term_out = (
        lax.dot_general(
            active_low, scaled_error, (((0,), (0,)), ((), ())), preferred_element_type=jnp.float32
        )
        * hidden ** (-0.5)
    ).astype(jnp.bfloat16)
    backward = lax.dot_general(
        scaled_error, full_out, (((1,), (1,)), ((), ())), preferred_element_type=jnp.float32
    ) * hidden ** (-0.5)
    grad_before = pullback(backward)[0].astype(jnp.bfloat16)
    term_in = (
        lax.dot_general(
            grad_before, frames_here, (((0,), (0,)), ((), ())), preferred_element_type=jnp.float32
        )
        * model_width ** (-0.5)
    ).astype(jnp.bfloat16)
    return (term_in, term_out)


ROOT_2_PI = 0.7978845608028654
CUBIC = 0.044715


def head_kernel(
    scale_error,
    frames_hbm, layers_hbm, mask_ref, w_in_ref, w_out_ref,
    grad_ref,
    frames, layers, target, full_in, full_out, active_t, slope_t, error, grad_t,
    term, pair_in, x_out, x_in, y_out, y_in, kept, half_kept, z_out, z_in, z_kept, whole,
    local_sem, w_send, w_recv, g_send, g_recv,
):
    f = lax.axis_index("fsdp")
    d = lax.axis_index("dp")
    x, c = f // 2, f % 2
    z, y = d // 2, d % 2
    sibling = {"dp": d, "fsdp": 2 * x + (1 - c)}
    x_peer = {"dp": d, "fsdp": 2 * (1 - x) + c}
    y_peer = {"dp": 2 * z + (1 - y), "fsdp": f}
    z_peers = [{"dp": 2 * ((z + j) % 4) + y, "fsdp": f} for j in (1, 2, 3)]
    across = [{"dp": 2 * ((z + j) % 4) + (1 - y), "fsdp": f} for j in (1, 2, 3)]
    far = 2 * (1 - x) + c

    loads = [
        pltpu.make_async_copy(layers_hbm, layers, local_sem.at[0]),
        pltpu.make_async_copy(frames_hbm, frames, local_sem.at[1]),
        pltpu.make_async_copy(w_in_ref, full_in.at[f], local_sem.at[2]),
        pltpu.make_async_copy(w_out_ref, full_out.at[f], local_sem.at[3]),
    ]
    for load in loads:
        load.start()

    barrier = pltpu.get_barrier_semaphore()
    peers = [sibling, x_peer, y_peer] + z_peers + across
    for peer in peers:
        pl.semaphore_signal(barrier, inc=1, device_id=peer, device_id_type=MESH)
    pl.semaphore_wait(barrier, len(peers))

    pending = []

    def remote(src, dst, send, recv, peer):
        copy = pltpu.make_async_remote_copy(
            src_ref=src, dst_ref=dst, send_sem=send, recv_sem=recv,
            device_id=peer, device_id_type=MESH,
        )
        copy.start()
        pending.append(copy)
        return copy

    near = [
        remote(w_in_ref, full_in.at[f], w_send.at[0, 0], w_recv.at[0, 0], sibling),
        remote(w_out_ref, full_out.at[f], w_send.at[1, 0], w_recv.at[1, 0], sibling),
    ]
    out_x = remote(w_out_ref.at[y], full_out.at[f, y], w_send.at[1, 1], w_recv.at[1, 1], x_peer)
    in_x = [
        remote(w_in_ref.at[h], full_in.at[f, h], w_send.at[0, 1 + h], w_recv.at[0, 1 + h], x_peer)
        for h in range(2)
    ]

    count, width = frames.shape
    def targets(first, last):
        for start in range(first, last, 128):
            total = None
            for layer in range(2):
                v = layers[layer, :, start:start + 128].astype(jnp.float32)
                center = v - jnp.mean(v, axis=0, keepdims=True)
                spread = jnp.mean(center * center, axis=0, keepdims=True)
                part = center * (0.5 / jnp.sqrt(spread + 1e-05))
                total = part if total is None else total + part
            target[:, start:start + 128] = total

    loads[0].wait()
    targets(0, width // 2)
    out_x.wait_recv()
    mine, other = full_out.at[far, y], full_out.at[far, 1 - y]
    out_y = remote(mine, mine, w_send.at[1, 2], w_recv.at[1, 2], y_peer)
    out_near = [remote(mine, mine, w_send.at[1, 3], w_recv.at[1, 3], sibling)]
    targets(width // 2, 3 * width // 4)
    in_near = []
    for h in range(2):
        in_x[h].wait_recv()
        piece = full_in.at[far, h]
        in_near.append(remote(piece, piece, w_send.at[0, 3 + h], w_recv.at[0, 3 + h], sibling))
        if h == 0:
            targets(3 * width // 4, width)
            block_of = lax.broadcasted_iota(jnp.int32, (count, mask_ref.shape[1]), 0) // SPAN
            hits = jnp.where(block_of == mask_ref[...], 1.0, 0.0)
            masked = jnp.max(hits, axis=1, keepdims=True)
    out_y.wait_recv()
    out_near.append(remote(other, other, w_send.at[1, 4], w_recv.at[1, 4], sibling))
    loads[1].wait()
    loads[2].wait()
    near[0].wait_recv()
    for copy in in_near:
        copy.wait_recv()

    hidden = 8 * full_in.shape[2]
    rows = hidden // 8
    in_all = full_in[...].reshape(hidden, width)
    before = lax.dot_general(
        in_all, frames[...], (((1,), (1,)), ((), ())), preferred_element_type=jnp.float32
    ) * width ** (-0.5)
    bend = jnp.tanh(ROOT_2_PI * (before + CUBIC * before * before * before))
    active_t[...] = (before * (0.5 * (1.0 + bend))).astype(jnp.bfloat16)
    slope_t[...] = 0.5 * (1.0 + bend) + (0.5 * ROOT_2_PI) * before * (1.0 - bend * bend) * (
        1.0 + 3.0 * CUBIC * before * before
    )

    loads[3].wait()
    near[1].wait_recv()
    for copy in out_near:
        copy.wait_recv()
    active = active_t[...].T

    half = width // 2

    def errors(start):
        for at in range(start, start + half, 256):
            predicted = jnp.dot(
                active, full_out[:, :, :, at:at + 256].reshape(hidden, 256),
                preferred_element_type=jnp.float32,
            ) * hidden ** (-0.5)
            error[:, at:at + 256] = (
                masked * (predicted - target[:, at:at + 256]) * scale_error
            ).astype(jnp.bfloat16)

    sent = {}

    def send_pair(s, value):
        value = value.astype(jnp.bfloat16)
        for i in range(8):
            term[s, i // 2, i % 2] = value[i * rows:(i + 1) * rows]
        sent[s, "pair"] = [
            remote(term.at[s, 2 * i + (1 - c)], pair_in.at[s, i], g_send.at[s, i], g_recv.at[s, i], sibling)
            for i in range(2)
        ]

    def wide(value):
        return value.astype(jnp.float32)

    def send_x(s, ref):
        return [remote(ref[0], ref[1], g_send.at[s, 2], g_recv.at[s, 2], x_peer)]

    def send_y(s, ref):
        return [remote(ref[0], ref[1], g_send.at[s, 3], g_recv.at[s, 3], y_peer)]

    def arrived(s, name):
        for copy in sent[s, name]:
            copy.wait_recv()

    def first(s):
        arrived(s, "pair")
        if s % 2 == 0:
            x_out[s] = (wide(term[s, far]) + wide(pair_in[s, 1 - x])).astype(jnp.bfloat16)
            sent[s, "first"] = send_x(s, (x_out.at[s], x_in.at[s]))
            kept[s] = wide(term[s, f]) + wide(pair_in[s, x])
        else:
            for i in range(2):
                y_out[s, i] = (
                    wide(term[s, 2 * i + c, 1 - y]) + wide(pair_in[s, i, 1 - y])
                ).astype(jnp.bfloat16)
            sent[s, "first"] = send_y(s, (y_out.at[s], y_in.at[s]))
            for i in range(2):
                kept[s, i] = wide(term[s, 2 * i + c, y]) + wide(pair_in[s, i, y])

    def second(s):
        arrived(s, "first")
        if s % 2 == 0:
            y_out[s, 0] = (kept[s, 1 - y] + wide(x_in[s, 1 - y])).astype(jnp.bfloat16)
            sent[s, "second"] = send_y(s, (y_out.at[s, 0], y_in.at[s, 0]))
            half_kept[s] = kept[s, y] + wide(x_in[s, y])
        else:
            x_out[s, 0] = (kept[s, 1 - x] + wide(y_in[s, 1 - x])).astype(jnp.bfloat16)
            sent[s, "second"] = send_x(s, (x_out.at[s, 0], x_in.at[s, 0]))
            half_kept[s] = kept[s, x] + wide(y_in[s, x])

    quarter = half // 4

    def third(s):
        arrived(s, "second")
        total = half_kept[s] + wide(y_in[s, 0] if s % 2 == 0 else x_in[s, 0])
        for q in range(4):
            part = total[:, q * quarter:(q + 1) * quarter]
            z_out[s, q] = part.astype(jnp.bfloat16)
            z_kept[s, q] = part
        sent[s, "third"] = [
            remote(
                z_out.at[s, (z + j) % 4], z_in.at[s, j - 1],
                g_send.at[s, 3 + j], g_recv.at[s, 3 + j], z_peers[j - 1],
            )
            for j in (1, 2, 3)
        ]

    def fourth(s):
        arrived(s, "third")
        total = z_kept[s, z] + wide(z_in[s, 0]) + wide(z_in[s, 1]) + wide(z_in[s, 2])
        whole[s, y, z] = total.astype(jnp.bfloat16)
        sent[s, "fourth"] = [
            remote(
                whole.at[s, y, z], whole.at[s, y, z],
                g_send.at[s, 6 + j], g_recv.at[s, 6 + j], z_peers[j - 1],
            )
            for j in (1, 2, 3)
        ]
        if s >= 2:
            sent[s, "fifth"] = [
                remote(
                    whole.at[s, y, z], whole.at[s, y, z],
                    g_send.at[s, 10 + j], g_recv.at[s, 10 + j], ([y_peer] + across)[j],
                )
                for j in range(4)
            ]

    def fifth(s):
        arrived(s, "fourth")
        if s >= 2:
            return
        sent[s, "fifth"] = [
            remote(whole.at[s, y], whole.at[s, y], g_send.at[s, 10], g_recv.at[s, 10], y_peer)
        ]

    def last(s):
        arrived(s, "fifth")
        for h in range(2):
            for q in range(4):
                at = (s % 2) * half + q * quarter
                grad_ref[s // 2, h * rows:(h + 1) * rows, at:at + quarter] = whole[s, h, q]

    for s in range(2):
        at = s * half
        errors(at)
        send_pair(
            s,
            jnp.dot(active_t[...], error[:, at:at + half], preferred_element_type=jnp.float32)
            * hidden ** (-0.5),
        )
    first(0)
    backward = lax.dot_general(
        full_out[...].reshape(hidden, width), error[...], (((1,), (1,)), ((), ())),
        preferred_element_type=jnp.float32,
    ) * hidden ** (-0.5)
    grad_t[...] = (slope_t[...] * backward).astype(jnp.bfloat16)
    first(1)
    for s in range(2, 4):
        at = (s - 2) * half
        send_pair(
            s,
            jnp.dot(grad_t[...], frames[:, at:at + half], preferred_element_type=jnp.float32)
            * width ** (-0.5),
        )
    first(2)
    first(3)
    for step in (second, third, fourth, fifth, last):
        for s in range(4):
            step(s)
    for copy in pending:
        copy.wait_send()


def head_call(student_frames, teacher_layers, mask_blocks, w_in, w_out, scale_error):
    count, width = student_frames.shape
    shard = w_in.shape[0]
    hidden = 4 * shard
    rows, half, quarter = shard // 2, width // 2, width // 8
    low, f32 = jnp.bfloat16, jnp.float32
    anywhere = pl.BlockSpec(memory_space=pl.ANY)
    inside = pl.BlockSpec(memory_space=pltpu.VMEM)
    return pl.pallas_call(
        functools.partial(head_kernel, scale_error),
        out_shape=jax.ShapeDtypeStruct((2, shard, width), low),
        in_specs=[anywhere, anywhere, inside, anywhere, anywhere],
        out_specs=inside,
        scratch_shapes=[
            pltpu.VMEM((count, width), low),
            pltpu.VMEM((2, count, width), low),
            pltpu.VMEM((count, width), f32),
            pltpu.VMEM((4, 2, rows, width), low),
            pltpu.VMEM((4, 2, rows, width), low),
            pltpu.VMEM((hidden, count), low),
            pltpu.VMEM((hidden, count), f32),
            pltpu.VMEM((count, width), low),
            pltpu.VMEM((hidden, count), low),
            pltpu.VMEM((4, 4, 2, rows, half), low),
            pltpu.VMEM((4, 2, 2, rows, half), low),
            pltpu.VMEM((4, 2, rows, half), low),
            pltpu.VMEM((4, 2, rows, half), low),
            pltpu.VMEM((4, 2, rows, half), low),
            pltpu.VMEM((4, 2, rows, half), low),
            pltpu.VMEM((4, 2, rows, half), f32),
            pltpu.VMEM((4, rows, half), f32),
            pltpu.VMEM((4, 4, rows, quarter), low),
            pltpu.VMEM((4, 3, rows, quarter), low),
            pltpu.VMEM((4, 4, rows, quarter), f32),
            pltpu.VMEM((4, 2, 4, rows, quarter), low),
            pltpu.SemaphoreType.DMA((4,)),
            pltpu.SemaphoreType.DMA((2, 5)),
            pltpu.SemaphoreType.DMA((2, 5)),
            pltpu.SemaphoreType.DMA((4, 14)),
            pltpu.SemaphoreType.DMA((4, 14)),
        ],
        compiler_params=pltpu.CompilerParams(
            collective_id=0, has_side_effects=True, vmem_limit_bytes=63 * 1024 * 1024
        ),
        cost_estimate=pl.CostEstimate(
            flops=10 * count * hidden * width,
            bytes_accessed=6 * count * width + 4 * hidden * width,
            transcendentals=count * hidden,
        ),
    )(
        student_frames, teacher_layers, mask_blocks,
        w_in.reshape(2, rows, width), w_out.reshape(2, rows, width),
    )


def averaged(w_in, w_out, teacher_in, teacher_out):
    ema_decay = 0.999
    new_in = ema_decay * teacher_in + (1.0 - ema_decay) * w_in.astype(jnp.float32)
    new_out = ema_decay * teacher_out + (1.0 - ema_decay) * w_out.astype(jnp.float32)
    return (new_in, new_out)


def body(student_frames, teacher_layers, mask_blocks, w_in, w_out, teacher_in, teacher_out):
    fused = lax.axis_size("fsdp") == 4 and lax.axis_size("dp") == 8
    if fused:
        total_masked = 32 * mask_blocks.shape[1] * SPAN
        grads = head_call(
            student_frames, teacher_layers, mask_blocks, w_in, w_out,
            (4 * w_in.shape[0] / total_masked) ** 0.5,
        ).astype(jnp.float32)
        return (grads[1], grads[0]) + averaged(w_in, w_out, teacher_in, teacher_out)
    full_in, full_out = (
        lax.all_gather(w_in, "fsdp", axis=0, tiled=True),
        lax.all_gather(w_out, "fsdp", axis=0, tiled=True),
    )
    count_dp = lax.axis_size("dp")
    count_fsdp = lax.axis_size("fsdp")
    total_masked = count_dp * count_fsdp * mask_blocks.shape[1] * SPAN
    term_in, term_out = local_terms(
        student_frames, teacher_layers, mask_blocks[0], full_in, full_out, total_masked
    )
    summands = (term_in.astype(jnp.float32), term_out.astype(jnp.float32))
    shards = (
        lax.psum_scatter(summands[0], "fsdp", scatter_dimension=0, tiled=True),
        lax.psum_scatter(summands[1], "fsdp", scatter_dimension=0, tiled=True),
    )
    grad_in, grad_out = lax.psum((shards[0], shards[1]), "dp")
    return (grad_in, grad_out) + averaged(w_in, w_out, teacher_in, teacher_out)


def solution(mesh):
    return jax.shard_map(
        body,
        mesh=mesh,
        in_specs=(
            P(("dp", "fsdp"), None),
            P(None, ("dp", "fsdp"), None),
            P(("dp", "fsdp"), None),
            P("fsdp", None),
            P("fsdp", None),
            P("fsdp", None),
            P("fsdp", None),
        ),
        out_specs=(P("fsdp", None), P("fsdp", None), P("fsdp", None), P("fsdp", None)),
        check_vma=False,
    )
```

```python
import functools

import jax
import jax.numpy as jnp
from jax import lax
from jax.experimental import pallas as pl
from jax.experimental.pallas import tpu as pltpu
from jax.sharding import PartitionSpec as P

MESH = pl.DeviceIdType.MESH

SPAN = 8


def gelu_fn(inputs):
    return jax.nn.gelu(inputs, approximate=True)


def targets_of(layers):
    values = layers.astype(jnp.float32)
    center = values - jnp.mean(values, axis=1, keepdims=True)
    spread = jnp.mean(center * center, axis=1, keepdims=True)
    return jnp.mean(center / jnp.sqrt(spread + 1e-05), axis=0)


def frame_mask(blocks, frames):
    block_of = jnp.arange(frames, dtype=jnp.int32) // SPAN
    matches = block_of[:, None] == blocks[None, :]
    return jnp.any(matches, axis=1).astype(jnp.float32)


def local_terms(frames_here, layers, blocks, full_in, full_out, total_masked):
    model_width = full_in.shape[1]
    hidden = full_in.shape[0]
    before = lax.dot_general(
        frames_here, full_in, (((1,), (1,)), ((), ())), preferred_element_type=jnp.float32
    ) * model_width ** (-0.5)
    active, pullback = jax.vjp(gelu_fn, before)
    active_low = active.astype(jnp.bfloat16)
    predicted = jnp.dot(active_low, full_out, preferred_element_type=jnp.float32) * hidden ** (-0.5)
    target = targets_of(layers)
    masked = frame_mask(blocks, frames_here.shape[0])
    scaled_error = (masked[:, None] * (predicted - target) * (hidden / total_masked) ** 0.5).astype(
        jnp.bfloat16
    )
    term_out = (
        lax.dot_general(
            active_low, scaled_error, (((0,), (0,)), ((), ())), preferred_element_type=jnp.float32
        )
        * hidden ** (-0.5)
    ).astype(jnp.bfloat16)
    backward = lax.dot_general(
        scaled_error, full_out, (((1,), (1,)), ((), ())), preferred_element_type=jnp.float32
    ) * hidden ** (-0.5)
    grad_before = pullback(backward)[0].astype(jnp.bfloat16)
    term_in = (
        lax.dot_general(
            grad_before, frames_here, (((0,), (0,)), ((), ())), preferred_element_type=jnp.float32
        )
        * model_width ** (-0.5)
    ).astype(jnp.bfloat16)
    return (term_in, term_out)


ROOT_2_PI = 0.7978845608028654
CUBIC = 0.044715


def head_kernel(
    scale_error,
    frames_hbm, layers_hbm, mask_ref, w_in_ref, w_out_ref,
    grad_ref,
    frames, layers, target, full_in, full_out, active_t, slope_t, error, grad_t,
    term, pair_in, x_out, x_in, y_out, y_in, kept, half_kept, z_out, z_in, z_kept, whole,
    local_sem, w_send, w_recv, g_send, g_recv,
):
    f = lax.axis_index("fsdp")
    d = lax.axis_index("dp")
    x, c = f // 2, f % 2
    z, y = d // 2, d % 2
    sibling = {"dp": d, "fsdp": 2 * x + (1 - c)}
    x_peer = {"dp": d, "fsdp": 2 * (1 - x) + c}
    y_peer = {"dp": 2 * z + (1 - y), "fsdp": f}
    z_peers = [{"dp": 2 * ((z + j) % 4) + y, "fsdp": f} for j in (1, 2, 3)]
    across = [{"dp": 2 * ((z + j) % 4) + (1 - y), "fsdp": f} for j in (1, 2, 3)]
    far = 2 * (1 - x) + c

    loads = [
        pltpu.make_async_copy(layers_hbm, layers, local_sem.at[0]),
        pltpu.make_async_copy(frames_hbm, frames, local_sem.at[1]),
        pltpu.make_async_copy(w_in_ref, full_in.at[f], local_sem.at[2]),
        pltpu.make_async_copy(w_out_ref, full_out.at[f], local_sem.at[3]),
    ]
    for load in loads:
        load.start()

    barrier = pltpu.get_barrier_semaphore()
    peers = [sibling, x_peer, y_peer] + z_peers + across
    for peer in peers:
        pl.semaphore_signal(barrier, inc=1, device_id=peer, device_id_type=MESH)
    pl.semaphore_wait(barrier, len(peers))

    pending = []

    def remote(src, dst, send, recv, peer):
        copy = pltpu.make_async_remote_copy(
            src_ref=src, dst_ref=dst, send_sem=send, recv_sem=recv,
            device_id=peer, device_id_type=MESH,
        )
        copy.start()
        pending.append(copy)
        return copy

    near = [
        remote(w_in_ref, full_in.at[f], w_send.at[0, 0], w_recv.at[0, 0], sibling),
        remote(w_out_ref, full_out.at[f], w_send.at[1, 0], w_recv.at[1, 0], sibling),
    ]
    out_x = remote(w_out_ref.at[y], full_out.at[f, y], w_send.at[1, 1], w_recv.at[1, 1], x_peer)
    in_x = [
        remote(w_in_ref.at[h], full_in.at[f, h], w_send.at[0, 1 + h], w_recv.at[0, 1 + h], x_peer)
        for h in range(2)
    ]

    count, width = frames.shape
    def targets(first, last):
        for start in range(first, last, 128):
            total = None
            for layer in range(2):
                v = layers[layer, :, start:start + 128].astype(jnp.float32)
                center = v - jnp.mean(v, axis=0, keepdims=True)
                spread = jnp.mean(center * center, axis=0, keepdims=True)
                part = center * (0.5 / jnp.sqrt(spread + 1e-05))
                total = part if total is None else total + part
            target[:, start:start + 128] = total

    loads[0].wait()
    targets(0, width // 2)
    out_x.wait_recv()
    mine, other = full_out.at[far, y], full_out.at[far, 1 - y]
    out_y = remote(mine, mine, w_send.at[1, 2], w_recv.at[1, 2], y_peer)
    out_near = [remote(mine, mine, w_send.at[1, 3], w_recv.at[1, 3], sibling)]
    targets(width // 2, 3 * width // 4)
    in_near = []
    for h in range(2):
        in_x[h].wait_recv()
        piece = full_in.at[far, h]
        in_near.append(remote(piece, piece, w_send.at[0, 3 + h], w_recv.at[0, 3 + h], sibling))
        if h == 0:
            targets(3 * width // 4, width)
            block_of = lax.broadcasted_iota(jnp.int32, (count, mask_ref.shape[1]), 0) // SPAN
            hits = jnp.where(block_of == mask_ref[...], 1.0, 0.0)
            masked = jnp.max(hits, axis=1, keepdims=True)
    out_y.wait_recv()
    out_near.append(remote(other, other, w_send.at[1, 4], w_recv.at[1, 4], sibling))
    loads[1].wait()
    loads[2].wait()
    near[0].wait_recv()
    for copy in in_near:
        copy.wait_recv()

    hidden = 8 * full_in.shape[2]
    rows = hidden // 8
    in_all = full_in[...].reshape(hidden, width)
    before = lax.dot_general(
        in_all, frames[...], (((1,), (1,)), ((), ())), preferred_element_type=jnp.float32
    ) * width ** (-0.5)
    bend = jnp.tanh(ROOT_2_PI * (before + CUBIC * before * before * before))
    active_t[...] = (before * (0.5 * (1.0 + bend))).astype(jnp.bfloat16)
    slope_t[...] = 0.5 * (1.0 + bend) + (0.5 * ROOT_2_PI) * before * (1.0 - bend * bend) * (
        1.0 + 3.0 * CUBIC * before * before
    )

    loads[3].wait()
    near[1].wait_recv()
    for copy in out_near:
        copy.wait_recv()
    active = active_t[...].T

    half = width // 2

    def errors(start):
        for at in range(start, start + half, 256):
            predicted = jnp.dot(
                active, full_out[:, :, :, at:at + 256].reshape(hidden, 256),
                preferred_element_type=jnp.float32,
            ) * hidden ** (-0.5)
            error[:, at:at + 256] = (
                masked * (predicted - target[:, at:at + 256]) * scale_error
            ).astype(jnp.bfloat16)

    sent = {}

    def send_pair(s, value):
        value = value.astype(jnp.bfloat16)
        for i in range(8):
            term[s, i // 2, i % 2] = value[i * rows:(i + 1) * rows]
        sent[s, "pair"] = [
            remote(term.at[s, 2 * i + (1 - c)], pair_in.at[s, i], g_send.at[s, i], g_recv.at[s, i], sibling)
            for i in range(2)
        ]

    def wide(value):
        return value.astype(jnp.float32)

    def send_x(s, ref):
        return [remote(ref[0], ref[1], g_send.at[s, 2], g_recv.at[s, 2], x_peer)]

    def send_y(s, ref):
        return [remote(ref[0], ref[1], g_send.at[s, 3], g_recv.at[s, 3], y_peer)]

    def arrived(s, name):
        for copy in sent[s, name]:
            copy.wait_recv()

    def first(s):
        arrived(s, "pair")
        if s % 2 == 0:
            x_out[s] = (wide(term[s, far]) + wide(pair_in[s, 1 - x])).astype(jnp.bfloat16)
            sent[s, "first"] = send_x(s, (x_out.at[s], x_in.at[s]))
            kept[s] = wide(term[s, f]) + wide(pair_in[s, x])
        else:
            for i in range(2):
                y_out[s, i] = (
                    wide(term[s, 2 * i + c, 1 - y]) + wide(pair_in[s, i, 1 - y])
                ).astype(jnp.bfloat16)
            sent[s, "first"] = send_y(s, (y_out.at[s], y_in.at[s]))
            for i in range(2):
                kept[s, i] = wide(term[s, 2 * i + c, y]) + wide(pair_in[s, i, y])

    def second(s):
        arrived(s, "first")
        if s % 2 == 0:
            y_out[s, 0] = (kept[s, 1 - y] + wide(x_in[s, 1 - y])).astype(jnp.bfloat16)
            sent[s, "second"] = send_y(s, (y_out.at[s, 0], y_in.at[s, 0]))
            half_kept[s] = kept[s, y] + wide(x_in[s, y])
        else:
            x_out[s, 0] = (kept[s, 1 - x] + wide(y_in[s, 1 - x])).astype(jnp.bfloat16)
            sent[s, "second"] = send_x(s, (x_out.at[s, 0], x_in.at[s, 0]))
            half_kept[s] = kept[s, x] + wide(y_in[s, x])

    quarter = half // 4

    def third(s):
        arrived(s, "second")
        total = half_kept[s] + wide(y_in[s, 0] if s % 2 == 0 else x_in[s, 0])
        for q in range(4):
            part = total[:, q * quarter:(q + 1) * quarter]
            z_out[s, q] = part.astype(jnp.bfloat16)
            z_kept[s, q] = part
        sent[s, "third"] = [
            remote(
                z_out.at[s, (z + j) % 4], z_in.at[s, j - 1],
                g_send.at[s, 3 + j], g_recv.at[s, 3 + j], z_peers[j - 1],
            )
            for j in (1, 2, 3)
        ]

    def fourth(s):
        arrived(s, "third")
        total = z_kept[s, z] + wide(z_in[s, 0]) + wide(z_in[s, 1]) + wide(z_in[s, 2])
        whole[s, y, z] = total.astype(jnp.bfloat16)
        sent[s, "fourth"] = [
            remote(
                whole.at[s, y, z], whole.at[s, y, z],
                g_send.at[s, 6 + j], g_recv.at[s, 6 + j], z_peers[j - 1],
            )
            for j in (1, 2, 3)
        ]
        if s >= 2:
            sent[s, "fifth"] = [
                remote(
                    whole.at[s, y, z], whole.at[s, y, z],
                    g_send.at[s, 10 + j], g_recv.at[s, 10 + j], ([y_peer] + across)[j],
                )
                for j in range(4)
            ]

    def fifth(s):
        arrived(s, "fourth")
        if s >= 2:
            return
        sent[s, "fifth"] = [
            remote(whole.at[s, y], whole.at[s, y], g_send.at[s, 10], g_recv.at[s, 10], y_peer)
        ]

    def last(s):
        arrived(s, "fifth")
        for h in range(2):
            for q in range(4):
                at = (s % 2) * half + q * quarter
                grad_ref[s // 2, h * rows:(h + 1) * rows, at:at + quarter] = whole[s, h, q]

    for s in range(2):
        at = s * half
        errors(at)
        send_pair(
            s,
            jnp.dot(active_t[...], error[:, at:at + half], preferred_element_type=jnp.float32)
            * hidden ** (-0.5),
        )
    first(0)
    backward = lax.dot_general(
        full_out[...].reshape(hidden, width), error[...], (((1,), (1,)), ((), ())),
        preferred_element_type=jnp.float32,
    ) * hidden ** (-0.5)
    grad_t[...] = (slope_t[...] * backward).astype(jnp.bfloat16)
    first(1)
    for s in range(2, 4):
        at = (s - 2) * half
        send_pair(
            s,
            jnp.dot(grad_t[...], frames[:, at:at + half], preferred_element_type=jnp.float32)
            * width ** (-0.5),
        )
    first(2)
    first(3)
    for step in (second, third, fourth, fifth, last):
        for s in range(4):
            step(s)
    for copy in pending:
        copy.wait_send()


def head_call(student_frames, teacher_layers, mask_blocks, w_in, w_out, scale_error):
    count, width = student_frames.shape
    shard = w_in.shape[0]
    hidden = 4 * shard
    rows, half, quarter = shard // 2, width // 2, width // 8
    low, f32 = jnp.bfloat16, jnp.float32
    anywhere = pl.BlockSpec(memory_space=pl.ANY)
    inside = pl.BlockSpec(memory_space=pltpu.VMEM)
    return pl.pallas_call(
        functools.partial(head_kernel, scale_error),
        out_shape=jax.ShapeDtypeStruct((2, shard, width), low),
        in_specs=[anywhere, anywhere, inside, anywhere, anywhere],
        out_specs=inside,
        scratch_shapes=[
            pltpu.VMEM((count, width), low),
            pltpu.VMEM((2, count, width), low),
            pltpu.VMEM((count, width), f32),
            pltpu.VMEM((4, 2, rows, width), low),
            pltpu.VMEM((4, 2, rows, width), low),
            pltpu.VMEM((hidden, count), low),
            pltpu.VMEM((hidden, count), f32),
            pltpu.VMEM((count, width), low),
            pltpu.VMEM((hidden, count), low),
            pltpu.VMEM((4, 4, 2, rows, half), low),
            pltpu.VMEM((4, 2, 2, rows, half), low),
            pltpu.VMEM((4, 2, rows, half), low),
            pltpu.VMEM((4, 2, rows, half), low),
            pltpu.VMEM((4, 2, rows, half), low),
            pltpu.VMEM((4, 2, rows, half), low),
            pltpu.VMEM((4, 2, rows, half), f32),
            pltpu.VMEM((4, rows, half), f32),
            pltpu.VMEM((4, 4, rows, quarter), low),
            pltpu.VMEM((4, 3, rows, quarter), low),
            pltpu.VMEM((4, 4, rows, quarter), f32),
            pltpu.VMEM((4, 2, 4, rows, quarter), low),
            pltpu.SemaphoreType.DMA((4,)),
            pltpu.SemaphoreType.DMA((2, 5)),
            pltpu.SemaphoreType.DMA((2, 5)),
            pltpu.SemaphoreType.DMA((4, 14)),
            pltpu.SemaphoreType.DMA((4, 14)),
        ],
        compiler_params=pltpu.CompilerParams(
            collective_id=0, has_side_effects=True, vmem_limit_bytes=62 * 1024 * 1024
        ),
        cost_estimate=pl.CostEstimate(
            flops=10 * count * hidden * width,
            bytes_accessed=6 * count * width + 4 * hidden * width,
            transcendentals=count * hidden,
        ),
    )(
        student_frames, teacher_layers, mask_blocks,
        w_in.reshape(2, rows, width), w_out.reshape(2, rows, width),
    )


def finish_kernel(grads, w_in, w_out, teacher_in, teacher_out, grad_in, grad_out, new_in, new_out):
    grad_in[...] = grads[1].astype(jnp.float32)
    grad_out[...] = grads[0].astype(jnp.float32)
    new_in[...], new_out[...] = averaged(w_in[...], w_out[...], teacher_in[...], teacher_out[...])


def finish_call(grads, w_in, w_out, teacher_in, teacher_out):
    shape = jax.ShapeDtypeStruct(teacher_in.shape, jnp.float32)
    inside = pl.BlockSpec(memory_space=pltpu.VMEM)
    return pl.pallas_call(
        finish_kernel,
        out_shape=[shape] * 4,
        in_specs=[inside] * 5,
        out_specs=[inside] * 4,
        compiler_params=pltpu.CompilerParams(vmem_limit_bytes=16 * 1024 * 1024),
    )(grads, w_in, w_out, teacher_in, teacher_out)


def averaged(w_in, w_out, teacher_in, teacher_out):
    ema_decay = 0.999
    new_in = ema_decay * teacher_in + (1.0 - ema_decay) * w_in.astype(jnp.float32)
    new_out = ema_decay * teacher_out + (1.0 - ema_decay) * w_out.astype(jnp.float32)
    return (new_in, new_out)


def body(student_frames, teacher_layers, mask_blocks, w_in, w_out, teacher_in, teacher_out):
    fused = lax.axis_size("fsdp") == 4 and lax.axis_size("dp") == 8
    if fused:
        total_masked = 32 * mask_blocks.shape[1] * SPAN
        low_grads = head_call(
            student_frames, teacher_layers, mask_blocks, w_in, w_out,
            (4 * w_in.shape[0] / total_masked) ** 0.5,
        )
        return tuple(finish_call(low_grads, w_in, w_out, teacher_in, teacher_out))
    full_in, full_out = (
        lax.all_gather(w_in, "fsdp", axis=0, tiled=True),
        lax.all_gather(w_out, "fsdp", axis=0, tiled=True),
    )
    count_dp = lax.axis_size("dp")
    count_fsdp = lax.axis_size("fsdp")
    total_masked = count_dp * count_fsdp * mask_blocks.shape[1] * SPAN
    term_in, term_out = local_terms(
        student_frames, teacher_layers, mask_blocks[0], full_in, full_out, total_masked
    )
    summands = (term_in.astype(jnp.float32), term_out.astype(jnp.float32))
    shards = (
        lax.psum_scatter(summands[0], "fsdp", scatter_dimension=0, tiled=True),
        lax.psum_scatter(summands[1], "fsdp", scatter_dimension=0, tiled=True),
    )
    grad_in, grad_out = lax.psum((shards[0], shards[1]), "dp")
    return (grad_in, grad_out) + averaged(w_in, w_out, teacher_in, teacher_out)


def solution(mesh):
    return jax.shard_map(
        body,
        mesh=mesh,
        in_specs=(
            P(("dp", "fsdp"), None),
            P(None, ("dp", "fsdp"), None),
            P(("dp", "fsdp"), None),
            P("fsdp", None),
            P("fsdp", None),
            P("fsdp", None),
            P("fsdp", None),
        ),
        out_specs=(P("fsdp", None), P("fsdp", None), P("fsdp", None), P("fsdp", None)),
        check_vma=False,
    )
```
